512 devices in a mesh: ctx: 16 (over z_lo, x), fsdp: 32 (over y, z_hi, core).
Axes of the slice: x: 4, y: 4, z: 16 (z_hi: 4, z_lo: 4; z = z_hi * 4 + z_lo), core: 2. Of those that a mesh axis runs over, the one named last changes fastest.
Arguments:
- queries: bfloat16 [6144, 4096], P('ctx', 'fsdp'), may hold values from -8 to 8
- keys: bfloat16 [6144, 4096], P('ctx', 'fsdp'), may hold values from -8 to 8
- values: bfloat16 [6144, 4096], P('ctx', 'fsdp'), may hold values from -6 to 6
- query_tangent: bfloat16 [6144, 4096], P('ctx', 'fsdp'), may hold values from -6 to 6
- key_tangent: bfloat16 [6144, 4096], P('ctx', 'fsdp'), may hold values from -6 to 6
- value_tangent: bfloat16 [6144, 4096], P('ctx', 'fsdp'), may hold values from -6 to 6
- out_weight: bfloat16 [4096, 5120], P('fsdp'), may hold values from -0.09375 to 0.09375
Outputs:
- projected: bfloat16 [6144, 5120], P('ctx', 'fsdp')
- projected_tangent: bfloat16 [6144, 5120], P('ctx', 'fsdp')
The draws below stay inside these ranges and needn't reach their ends.
All inputs are finite; a program needn't handle non-finite values.
Results may differ from the reference program's by a relative error of at most 0.024.
Values may be sent and summed in bfloat16 or wider, within the bound.
A program may use at most 128 MiB of HBM per device.

```python
import jax
import jax.numpy as jnp
from jax import lax

HEADS = 32
HD = 128
DOUT = 5120
FEAT = 4096
SEQ = 6144


def keys_common(key):
    return jax.random.normal(key, (SEQ, FEAT), jnp.float32)


def draw_keys(key, part):
    base = jnp.clip(keys_common(key), -4.0, 4.0)
    out = base
    return out.astype(jnp.bfloat16)


def draw_queries(key, part):
    key = jax.random.fold_in(key, 7)
    out = jax.random.normal(key, (SEQ, FEAT), jnp.float32)
    return jnp.clip(out, -8.0, 8.0).astype(jnp.bfloat16)


def block_scale(stream_key, dims, pieces, low, high):
    def one(dim, shards_of):
        steps = jax.random.uniform(jax.random.fold_in(jax.random.fold_in(stream_key, 6), dim), (shards_of,), jnp.float32, low / len(pieces), high / len(pieces))
        return jnp.repeat(jnp.exp(steps), dims[dim] // shards_of).reshape((-1,) + (1,) * (len(dims) - dim - 1))

    factor_of = one(*pieces[0])
    for cut in pieces[1:]:
        factor_of = factor_of * one(*cut)
    return factor_of


def bell_draw(key, dims, deviation, bound, cuts=(), kind=jnp.bfloat16):
    values = deviation * jax.random.normal(key, dims, jnp.float32)
    if cuts:
        values = values * block_scale(key, dims, cuts, -0.22, 0.18)
    return jnp.clip(values, -bound, bound).astype(kind)


def setup_inputs(seed: int = 0) -> dict:
    key_of = jax.random.split(jax.random.key(seed), 8)
    return {
        "queries": draw_queries(jax.random.fold_in(key_of[7], 71), 0),
        "keys": draw_keys(jax.random.fold_in(key_of[7], 71), 0),
        "values": bell_draw(key_of[2], (SEQ, FEAT), 1.0, 6.0, ((0, 16), (1, 32))),
        "query_tangent": bell_draw(key_of[3], (SEQ, FEAT), 1.0, 6.0, ((0, 16), (1, 32))),
        "key_tangent": bell_draw(key_of[4], (SEQ, FEAT), 1.0, 6.0, ((0, 16), (1, 32))),
        "value_tangent": bell_draw(key_of[5], (SEQ, FEAT), 1.0, 6.0, ((0, 16), (1, 32))),
        "out_weight": bell_draw(key_of[6], (FEAT, DOUT), FEAT ** -0.5, 0.09375, ((0, 32),)),
    }


def attend_head(entry_list):
    query_flat, key_flat, value_flat, query_tangent_flat, key_tangent_flat, value_tangent_flat = [attention_probs.astype(jnp.float32) for attention_probs in entry_list]
    scale = 1.0 / (HD ** 0.5)
    scores = jnp.dot(query_flat, key_flat.T) * scale
    score_tangent = (jnp.dot(query_tangent_flat, key_flat.T) + jnp.dot(query_flat, key_tangent_flat.T)) * scale
    top = jnp.max(scores, axis=-1, keepdims=True)
    weights = jnp.exp(scores - top)
    total = jnp.sum(weights, axis=-1)
    spread = weights * score_tangent
    spread_total = jnp.sum(spread, axis=-1)
    weights_reduced = weights.astype(jnp.bfloat16).astype(jnp.float32)
    spread_reduced = spread.astype(jnp.bfloat16).astype(jnp.float32)
    primal_sum = jnp.dot(weights_reduced, value_flat)
    summed_tangent_block = jnp.dot(weights_reduced, value_tangent_flat) + jnp.dot(spread_reduced, value_flat)
    mixed = primal_sum / total[:, None]
    mixed_tangent = summed_tangent_block / total[:, None] - (spread_total / total)[:, None] * mixed
    return mixed.astype(jnp.bfloat16), mixed_tangent.astype(jnp.bfloat16)


def reference(queries, keys, values, query_tangent, key_tangent, value_tangent, out_weight):
    entry_list = tuple(jnp.transpose(attention_probs.reshape(SEQ, HEADS, HD), (1, 0, 2)) for attention_probs in (queries, keys, values, query_tangent, key_tangent, value_tangent))
    mixed, mixed_tangent = lax.map(attend_head, entry_list)
    mixed = jnp.transpose(mixed, (1, 0, 2)).reshape(SEQ, FEAT)
    mixed_tangent = jnp.transpose(mixed_tangent, (1, 0, 2)).reshape(SEQ, FEAT)
    projected = jnp.dot(mixed, out_weight, preferred_element_type=jnp.float32).astype(jnp.bfloat16)
    projected_tangent = jnp.dot(mixed_tangent, out_weight, preferred_element_type=jnp.float32).astype(jnp.bfloat16)
    return (projected, projected_tangent)
```

```python
import functools

import jax
import jax.numpy as jnp
from jax import lax
from jax.experimental import pallas as pl
from jax.experimental.pallas import tpu as pltpu
from jax.sharding import PartitionSpec as P

MESH = pl.DeviceIdType.MESH
HD = 128
F32 = jnp.float32
BF16 = jnp.bfloat16
DIMS = (4, 4, 4, 4, 2)


def nt_dot(a, b):
    return lax.dot_general(a, b, (((1,), (1,)), ((), ())), preferred_element_type=F32)


def kernel(
    dims,
    q_ref, k_ref, v_ref, dq_ref, dk_ref, dv_ref, w_ref,
    out_ref, dout_ref,
    qd_all, kd_all, vt_own, vt_all, wt_own, wt_all,
    part, stats, part_in, stats_in, mix, x_all, send_z, recv_z, swap_out, swap_in,
    q_s, q_r, k_s, k_r, v_s, v_r, w_s, w_r, p_s, p_r, t_s, t_r, x_s, x_r, z_s, z_r, c_s, c_r, l_s,
):
    nx, nz, ny, nh, nc = dims
    tok = q_ref.shape[0]
    col = out_ref.shape[1]
    scale = 1.0 / HD**0.5
    rate = scale * 1.4426950408889634

    ctx = lax.axis_index("ctx")
    fsdp = lax.axis_index("fsdp")
    zl, x = ctx // nx, lax.rem(ctx, nx)
    core = lax.rem(fsdp, nc)
    zh = lax.rem(fsdp // nc, nh)
    y = fsdp // (nc * nh)

    def at_x(d):
        return (zl * nx + lax.rem(x + d, nx), fsdp)

    def at_zl(d):
        return (lax.rem(zl + d, nz) * nx + x, fsdp)

    def at_zh(d):
        return (ctx, (y * nh + lax.rem(zh + d, nh)) * nc + core)

    def at_yc(e):
        return (ctx, (lax.rem(y + e // nc, ny) * nh + zh) * nc + lax.rem(core + e % nc, nc))

    partners = (
        [at_x(d) for d in range(1, nx)]
        + [at_zl(d) for d in range(1, nz)]
        + [at_zh(d) for d in range(1, nh)]
        + [at_yc(e) for e in range(1, ny * nc)]
    )
    barrier = pltpu.get_barrier_semaphore()
    for device in partners:
        pl.semaphore_signal(barrier, inc=1, device_id=device, device_id_type=MESH)

    key_rows = pl.ds(pl.multiple_of(x * tok, tok), tok)
    kd_all[key_rows, 0:HD] = k_ref[...]
    kd_all[key_rows, HD : 2 * HD] = dk_ref[...]
    qd_all[zl, :, 0:HD] = dq_ref[...]
    qd_all[zl, :, HD : 2 * HD] = q_ref[...]
    vt_own[0:HD, :] = v_ref[...].T
    vt_own[HD : 2 * HD, :] = dv_ref[...].T

    pl.semaphore_wait(barrier, len(partners))

    def remote(src, dst, s, r, device):
        return pltpu.make_async_remote_copy(
            src_ref=src, dst_ref=dst, send_sem=s, recv_sem=r, device_id=device, device_id_type=MESH
        )

    q_copies = [
        remote(qd_all.at[zl], qd_all.at[zl], q_s.at[d - 1], q_r.at[d - 1], at_zl(d))
        for d in range(1, nz)
    ]
    k_copies = [
        remote(kd_all.at[key_rows], kd_all.at[key_rows], k_s.at[d - 1], k_r.at[d - 1], at_x(d))
        for d in range(1, nx)
    ]
    v_copies = [
        remote(vt_own, vt_all.at[:, key_rows], v_s.at[d - 1], v_r.at[d - 1], at_x(d))
        for d in range(1, nx)
    ]
    for copy in q_copies + k_copies + v_copies:
        copy.start()
    v_local = pltpu.make_async_copy(vt_own, vt_all.at[:, key_rows], l_s.at[0])
    v_local.start()

    group = nh * nc * col
    for i in range(ny):
        wt_own[i * group : (i + 1) * group, :] = w_ref[:, i * group : (i + 1) * group].T
    slot = y * nc + core
    slot_cols = pl.ds(pl.multiple_of(slot * HD, HD), HD)

    def weight_rows(row):
        return pl.ds(pl.multiple_of(row * group, group), group)

    w_copies = [
        remote(
            wt_own.at[weight_rows(lax.rem(y + e // nc, ny))],
            wt_all.at[:, slot_cols],
            w_s.at[e - 1],
            w_r.at[e - 1],
            at_yc(e),
        )
        for e in range(1, ny * nc)
    ]
    for copy in w_copies:
        copy.start()
    w_local = pltpu.make_async_copy(wt_own.at[weight_rows(y)], wt_all.at[:, slot_cols], l_s.at[1])
    w_local.start()

    for copy in q_copies + k_copies + v_copies:
        copy.wait()
    v_local.wait()

    def attend(j, carry):
        owner = lax.rem(zl + j + 1, nz)
        qd = qd_all[owner]
        scores = nt_dot(kd_all[:, 0:HD], qd[:, HD : 2 * HD])
        steps = nt_dot(kd_all[...], qd)
        top = jnp.max(scores, axis=0, keepdims=True)
        weights = jnp.exp2((scores - top) * rate)
        spread = weights * steps
        total = jnp.sum(weights, axis=0, keepdims=True)
        mean = jnp.sum(spread, axis=0, keepdims=True) * scale / total
        first = jnp.dot(vt_all[...], weights.astype(BF16), preferred_element_type=F32)
        second = jnp.dot(vt_all[0:HD, :], spread.astype(BF16), preferred_element_type=F32)
        mixed = first[0:HD] / total
        part[j, 0:HD, :] = mixed.astype(BF16)
        part[j, HD : 2 * HD, :] = (
            (first[HD : 2 * HD] + second * scale) / total - mean * mixed
        ).astype(BF16)
        stats[j, 0:1, :] = top * rate
        stats[j, 1:2, :] = total
        stats[j, 2:3, :] = mean
        stats[j, 3:8, :] = jnp.zeros((5, tok), F32)

        @pl.when(j < nz - 1)
        def _():
            device = (owner * nx + x, fsdp)
            remote(part.at[j], part_in.at[j], p_s.at[j], p_r.at[j], device).start()
            remote(stats.at[j], stats_in.at[j], t_s.at[j], t_r.at[j], device).start()

        return carry

    lax.fori_loop(0, nz, attend, 0)

    for j in range(nz - 1):
        remote(part.at[j], part_in.at[j], p_s.at[j], p_r.at[j], at_zl(j + 1)).wait()
        remote(stats.at[j], stats_in.at[j], t_s.at[j], t_r.at[j], at_zl(j + 1)).wait()

    parts = [(part_in.at[j], stats_in.at[j]) for j in range(nz - 1)]
    parts.append((part.at[nz - 1], stats.at[nz - 1]))
    tops = [s[0:1, :] for _, s in parts]
    top = functools.reduce(jnp.maximum, tops)
    shares = [jnp.exp2(t - top) * s[1:2, :] for t, (_, s) in zip(tops, parts)]
    total = sum(shares)
    shares = [s / total for s in shares]
    means = [s[2:3, :] for _, s in parts]
    mean = sum(a * b for a, b in zip(shares, means))
    mixed = jnp.zeros((HD, tok), F32)
    tangent = jnp.zeros((HD, tok), F32)
    for share, here, (p, _) in zip(shares, means, parts):
        one = p[0:HD, :].astype(F32)
        mixed += share * one
        tangent += share * (p[HD : 2 * HD, :].astype(F32) + (here - mean) * one)
    mix[0] = mixed.astype(BF16)
    mix[1] = tangent.astype(BF16)

    slot_rows = pl.ds(pl.multiple_of(slot * HD, HD), HD)
    x_copies = [
        remote(
            mix.at[lax.rem(core + e % nc, nc)],
            x_all.at[slot_rows],
            x_s.at[e - 1],
            x_r.at[e - 1],
            at_yc(e),
        )
        for e in range(1, ny * nc)
    ]
    for copy in x_copies:
        copy.start()
    x_all[slot_rows, :] = mix[core]
    for copy in w_copies + x_copies:
        copy.wait()
    w_local.wait()

    block = nc * col

    def project(d):
        rows = pl.ds(pl.multiple_of(lax.rem(zh + d, nh) * block, block), block)
        return jnp.dot(wt_all[rows, :], x_all[...], preferred_element_type=F32)

    z_copies = []
    for d in range(1, nh):
        send_z[d - 1] = project(d).astype(BF16)
        copy = remote(send_z.at[d - 1], recv_z.at[d - 1], z_s.at[d - 1], z_r.at[d - 1], at_zh(d))
        copy.start()
        z_copies.append(copy)
    total = project(0)
    for d in range(1, nh):
        z_copies[d - 1].wait()
        total += recv_z[d - 1].astype(F32)
    swap_out[...] = total.astype(BF16)

    other = lax.rem(core + 1, nc)

    def cols(c):
        return pl.ds(pl.multiple_of(c * col, col), col)

    copy = remote(swap_out.at[cols(other)], swap_in, c_s, c_r, at_yc(1))
    copy.start()
    mine = swap_out[cols(core), :]
    copy.wait()
    theirs = swap_in[...]
    out_ref[...] = jnp.where(core == 0, mine, theirs).T
    dout_ref[...] = jnp.where(core == 0, theirs, mine).T


def call(dims, q, k, v, dq, dk, dv, w):
    nx, nz, ny, nh, nc = dims
    tok = q.shape[0]
    col = w.shape[1] // (ny * nh * nc)
    block = nc * col
    group = nh * block
    peers = ny * nc
    dma = pltpu.SemaphoreType.DMA
    vmem = pl.BlockSpec(memory_space=pltpu.VMEM)

    def pair(n):
        return [dma((max(n, 1),)), dma((max(n, 1),))]

    return pl.pallas_call(
        functools.partial(kernel, dims),
        out_shape=(
            jax.ShapeDtypeStruct((tok, col), BF16),
            jax.ShapeDtypeStruct((tok, col), BF16),
        ),
        in_specs=[vmem] * 7,
        out_specs=(vmem, vmem),
        scratch_shapes=[
            pltpu.VMEM((nz, tok, 2 * HD), BF16),
            pltpu.VMEM((nx * tok, 2 * HD), BF16),
            pltpu.VMEM((2 * HD, tok), BF16),
            pltpu.VMEM((2 * HD, nx * tok), BF16),
            pltpu.VMEM((w.shape[1], HD), BF16),
            pltpu.VMEM((group, peers * HD), BF16),
            pltpu.VMEM((nz, 2 * HD, tok), BF16),
            pltpu.VMEM((nz, 8, tok), F32),
            pltpu.VMEM((max(nz - 1, 1), 2 * HD, tok), BF16),
            pltpu.VMEM((max(nz - 1, 1), 8, tok), F32),
            pltpu.VMEM((2, HD, tok), BF16),
            pltpu.VMEM((peers * HD, tok), BF16),
            pltpu.VMEM((max(nh - 1, 1), block, tok), BF16),
            pltpu.VMEM((max(nh - 1, 1), block, tok), BF16),
            pltpu.VMEM((block, tok), BF16),
            pltpu.VMEM((col, tok), BF16),
        ]
        + pair(nz - 1)
        + pair(nx - 1)
        + pair(nx - 1)
        + pair(peers - 1)
        + pair(nz - 1)
        + pair(nz - 1)
        + pair(peers - 1)
        + pair(nh - 1)
        + [dma, dma, dma((2,))],
        compiler_params=pltpu.CompilerParams(
            collective_id=0, has_side_effects=True, vmem_limit_bytes=56 * 1024 * 1024
        ),
        name="attend_and_project",
    )(q, k, v, dq, dk, dv, w)


def solution(mesh, dims=DIMS):
    spec = P("ctx", "fsdp")
    return jax.shard_map(
        functools.partial(call, dims),
        mesh=mesh,
        in_specs=(spec,) * 6 + (P("fsdp", None),),
        out_specs=(spec, spec),
        check_vma=False,
    )
```

```python
import functools

import jax
import jax.numpy as jnp
from jax import lax
from jax.experimental import pallas as pl
from jax.experimental.pallas import tpu as pltpu
from jax.sharding import PartitionSpec as P

MESH = pl.DeviceIdType.MESH
HD = 128
F32 = jnp.float32
BF16 = jnp.bfloat16
DIMS = (4, 4, 4, 4, 2)


def nt_dot(a, b):
    return lax.dot_general(a, b, (((1,), (1,)), ((), ())), preferred_element_type=F32)


def kernel(
    dims, chunks,
    q_ref, k_ref, v_ref, dq_ref, dk_ref, dv_ref, w_ref,
    out_ref, dout_ref,
    qd_all, kd_all, v_in, vt_own, vt_all, w_in, wt_own, wt_all,
    part, stats, part_in, stats_in, mix, x_all, send_z, recv_z, hold_a, hold_b, own, swap_out, swap_in,
    q_s, q_r, k_s, k_r, v_s, v_r, w_s, w_r, p_s, p_r, t_s, t_r, x_s, x_r, z_s, z_r, c_s, c_r, l_s,
):
    nx, nz, ny, nh, nc = dims
    tok = q_ref.shape[0]
    col = out_ref.shape[1]
    scale = 1.0 / HD**0.5
    rate = scale * 1.4426950408889634

    ctx = lax.axis_index("ctx")
    fsdp = lax.axis_index("fsdp")
    zl, x = ctx // nx, lax.rem(ctx, nx)
    core = lax.rem(fsdp, nc)
    zh = lax.rem(fsdp // nc, nh)
    y = fsdp // (nc * nh)

    def at_x(d):
        return (zl * nx + lax.rem(x + d, nx), fsdp)

    def at_zl(d):
        return (lax.rem(zl + d, nz) * nx + x, fsdp)

    def at_zh(d):
        return (ctx, (y * nh + lax.rem(zh + d, nh)) * nc + core)

    def at_yc(e):
        return (ctx, (lax.rem(y + e // nc, ny) * nh + zh) * nc + lax.rem(core + e % nc, nc))

    partners = (
        [at_x(d) for d in range(1, nx)]
        + [at_zl(d) for d in range(1, nz)]
        + [at_zh(1), at_zh(nh - 1)]
        + [at_yc(e) for e in range(1, ny * nc)]
    )
    barrier = pltpu.get_barrier_semaphore()
    for device in partners:
        pl.semaphore_signal(barrier, inc=1, device_id=device, device_id_type=MESH)

    def remote(src, dst, s, r, device):
        return pltpu.make_async_remote_copy(
            src_ref=src, dst_ref=dst, send_sem=s, recv_sem=r, device_id=device, device_id_type=MESH
        )

    key_rows = pl.ds(pl.multiple_of(x * tok, tok), tok)
    first, second = slice(0, HD), slice(HD, 2 * HD)
    local = [
        pltpu.make_async_copy(src, dst, l_s.at[i])
        for i, (src, dst) in enumerate(
            [
                (v_ref, v_in.at[0]),
                (dv_ref, v_in.at[1]),
                (dq_ref, qd_all.at[zl, :, first]),
                (q_ref, qd_all.at[zl, :, second]),
                (k_ref, kd_all.at[key_rows, first]),
                (dk_ref, kd_all.at[key_rows, second]),
                (w_ref, w_in),
            ]
        )
    ]
    for copy in local:
        copy.start()
    for copy in local[:2]:
        copy.wait()
    vt_own[first, :] = v_in[0].T
    vt_own[second, :] = v_in[1].T
    for copy in local[2:6]:
        copy.wait()

    pl.semaphore_wait(barrier, len(partners))

    q_copies = [
        remote(qd_all.at[zl], qd_all.at[zl], q_s.at[d - 1], q_r.at[d - 1], at_zl(d))
        for d in range(1, nz)
    ]
    k_copies = [
        remote(kd_all.at[key_rows], kd_all.at[key_rows], k_s.at[d - 1], k_r.at[d - 1], at_x(d))
        for d in range(1, nx)
    ]
    v_copies = [
        remote(vt_own, vt_all.at[:, key_rows], v_s.at[d - 1], v_r.at[d - 1], at_x(d))
        for d in range(1, nx)
    ]
    for copy in q_copies + k_copies + v_copies:
        copy.start()
    v_local = pltpu.make_async_copy(vt_own, vt_all.at[:, key_rows], l_s.at[0])
    v_local.start()

    group = nh * nc * col
    local[6].wait()
    for i in range(ny):
        wt_own[i * group : (i + 1) * group, :] = w_in[:, i * group : (i + 1) * group].T
    slot = y * nc + core
    slot_cols = pl.ds(pl.multiple_of(slot * HD, HD), HD)

    def weight_rows(row):
        return pl.ds(pl.multiple_of(row * group, group), group)

    w_copies = [
        remote(
            wt_own.at[weight_rows(lax.rem(y + e // nc, ny))],
            wt_all.at[:, slot_cols],
            w_s.at[e - 1],
            w_r.at[e - 1],
            at_yc(e),
        )
        for e in range(1, ny * nc)
    ]
    for copy in w_copies:
        copy.start()
    w_local = pltpu.make_async_copy(wt_own.at[weight_rows(y)], wt_all.at[:, slot_cols], l_s.at[1])
    w_local.start()

    for copy in q_copies + k_copies + v_copies:
        copy.wait()
    v_local.wait()

    def part_copies(c, lanes, j, device):
        i = c * (nz - 1) + j
        return (
            remote(part.at[j, :, lanes], part_in.at[j, :, lanes], p_s.at[i], p_r.at[i], device),
            remote(stats.at[j, :, lanes], stats_in.at[j, :, lanes], t_s.at[i], t_r.at[i], device),
        )

    for c, (at, size) in enumerate(chunks):
        lanes = slice(at, at + size)

        def attend(j, carry):
            owner = lax.rem(zl + j + 1, nz)
            qd = qd_all[owner, lanes, :]
            scores = nt_dot(kd_all[:, first], qd[:, second])
            steps = nt_dot(kd_all[...], qd)
            top = jnp.max(scores, axis=0, keepdims=True)
            weights = jnp.exp2((scores - top) * rate)
            spread = weights * steps
            total = jnp.sum(weights, axis=0, keepdims=True)
            mean = jnp.sum(spread, axis=0, keepdims=True) * scale / total
            low = weights.astype(BF16)
            one = jnp.dot(vt_all[...], low, preferred_element_type=F32)
            two = jnp.dot(vt_all[first, :], spread.astype(BF16), preferred_element_type=F32)
            mixed = one[first] / total
            part[j, first, lanes] = mixed.astype(BF16)
            part[j, second, lanes] = ((one[second] + two * scale) / total - mean * mixed).astype(
                BF16
            )
            stats[j, 0:1, lanes] = top * rate
            stats[j, 1:2, lanes] = total
            stats[j, 2:3, lanes] = mean
            stats[j, 3:8, lanes] = jnp.zeros((5, size), F32)

            @pl.when(j < nz - 1)
            def _():
                for copy in part_copies(c, lanes, j, (owner * nx + x, fsdp)):
                    copy.start()

            return carry

        lax.fori_loop(0, nz, attend, 0)

    block = nc * col
    slot_rows = pl.ds(pl.multiple_of(slot * HD, HD), HD)
    top_half, low_half = slice(0, block // 2), slice(block // 2, block)
    other = lax.rem(core + 1, nc)

    def merge(c):
        at, size = chunks[c]
        lanes = slice(at, at + size)
        for j in range(nz - 1):
            for copy in part_copies(c, lanes, j, at_zl(j + 1)):
                copy.wait()
        parts = [(part_in.at[j], stats_in.at[j]) for j in range(nz - 1)]
        parts.append((part.at[nz - 1], stats.at[nz - 1]))
        tops = [s[0:1, lanes] for _, s in parts]
        top = functools.reduce(jnp.maximum, tops)
        shares = [jnp.exp2(t - top) * s[1:2, lanes] for t, (_, s) in zip(tops, parts)]
        total = sum(shares)
        shares = [s / total for s in shares]
        means = [s[2:3, lanes] for _, s in parts]
        mean = sum(a * b for a, b in zip(shares, means))
        mixed = jnp.zeros((HD, size), F32)
        tangent = jnp.zeros((HD, size), F32)
        for share, here, (p, _) in zip(shares, means, parts):
            one = p[first, lanes].astype(F32)
            mixed += share * one
            tangent += share * (p[second, lanes].astype(F32) + (here - mean) * one)
        mix[0, :, lanes] = mixed.astype(BF16)
        mix[1, :, lanes] = tangent.astype(BF16)
        n = ny * nc - 1
        copies = [
            remote(
                mix.at[lax.rem(core + e % nc, nc), :, lanes],
                x_all.at[slot_rows, lanes],
                x_s.at[c * n + e - 1],
                x_r.at[c * n + e - 1],
                at_yc(e),
            )
            for e in range(1, ny * nc)
        ]
        for copy in copies:
            copy.start()
        x_all[slot_rows, lanes] = mix[core, :, lanes]
        return copies

    def z_copy(c, i, d):
        at, size = chunks[c]
        lanes = slice(at, at + size)
        k = 6 * c + i
        return remote(
            send_z.at[i, :, lanes], recv_z.at[i, :, lanes], z_s.at[k], z_r.at[k], at_zh(d)
        )

    def project(c):
        at, size = chunks[c]
        lanes = slice(at, at + size)

        def dot(d):
            rows = pl.ds(pl.multiple_of(lax.rem(zh + d, nh) * block, block), block)
            return jnp.dot(wt_all[rows, :], x_all[:, lanes], preferred_element_type=F32)

        far = dot(2)
        send_z[0, :, lanes] = far[top_half].astype(BF16)
        send_z[1, :, lanes] = far[low_half].astype(BF16)
        copies = [z_copy(c, 0, 1), z_copy(c, 1, 3)]
        for copy in copies:
            copy.start()
        after = dot(1)
        hold_a[:, lanes] = after[top_half]
        send_z[2, :, lanes] = after[low_half].astype(BF16)
        copies.append(z_copy(c, 2, 1))
        copies[2].start()
        before = dot(3)
        hold_b[:, lanes] = before[low_half]
        send_z[3, :, lanes] = before[top_half].astype(BF16)
        copies.append(z_copy(c, 3, 3))
        copies[3].start()
        own[:, lanes] = dot(0)
        return copies

    def forward(c, copies):
        at, size = chunks[c]
        lanes = slice(at, at + size)
        for i, hold, d in ((0, hold_a, 1), (1, hold_b, 3)):
            copies[i].wait()
            send_z[4 + i, :, lanes] = (hold[:, lanes] + recv_z[i, :, lanes].astype(F32)).astype(
                BF16
            )
            copies.append(z_copy(c, 4 + i, d))
            copies[4 + i].start()

    def cols(i):
        return pl.ds(pl.multiple_of(i * col, col), col)

    def finish(c, copies):
        at, size = chunks[c]
        lanes = slice(at, at + size)
        for copy in copies[2:]:
            copy.wait()
        for rows, i, j in ((top_half, 3, 4), (low_half, 2, 5)):
            total = own[rows, lanes] + recv_z[i, :, lanes].astype(F32)
            swap_out[rows, lanes] = (total + recv_z[j, :, lanes].astype(F32)).astype(BF16)
        copy = remote(
            swap_out.at[cols(other), lanes], swap_in.at[:, lanes], c_s.at[c], c_r.at[c], at_yc(1)
        )
        copy.start()
        return copy

    def write(c, copy):
        at, size = chunks[c]
        lanes = slice(at, at + size)
        mine = swap_out[cols(core), lanes]
        copy.wait()
        theirs = swap_in[:, lanes]
        out_ref[lanes, :] = jnp.where(core == 0, mine, theirs).T
        dout_ref[lanes, :] = jnp.where(core == 0, theirs, mine).T

    last = len(chunks) - 1
    sends = {}
    for c in range(last + 1):
        x_copies = merge(c)
        if c > 0:
            forward(c - 1, sends[c - 1])
        if c == 0:
            for copy in w_copies:
                copy.wait()
            w_local.wait()
        for copy in x_copies:
            copy.wait()
        sends[c] = project(c)
    swaps = {c: finish(c, sends[c]) for c in range(last)}
    forward(last, sends[last])
    for c in range(last):
        write(c, swaps[c])
    write(last, finish(last, sends[last]))


def call(dims, q, k, v, dq, dk, dv, w):
    nx, nz, ny, nh, nc = dims
    tok = q.shape[0]
    col = w.shape[1] // (ny * nh * nc)
    block = nc * col
    group = nh * block
    peers = ny * nc
    chunks = ((0, HD), (HD, tok - HD))
    n = len(chunks)
    dma = pltpu.SemaphoreType.DMA
    vmem = pl.BlockSpec(memory_space=pltpu.VMEM)

    def pair(n):
        return [dma((max(n, 1),)), dma((max(n, 1),))]

    return pl.pallas_call(
        functools.partial(kernel, dims, chunks),
        out_shape=(
            jax.ShapeDtypeStruct((tok, col), BF16),
            jax.ShapeDtypeStruct((tok, col), BF16),
        ),
        in_specs=[pl.BlockSpec(memory_space=pl.ANY)] * 7,
        out_specs=(vmem, vmem),
        scratch_shapes=[
            pltpu.VMEM((nz, tok, 2 * HD), BF16),
            pltpu.VMEM((nx * tok, 2 * HD), BF16),
            pltpu.VMEM((2, tok, HD), BF16),
            pltpu.VMEM((2 * HD, tok), BF16),
            pltpu.VMEM((2 * HD, nx * tok), BF16),
            pltpu.VMEM(w.shape, BF16),
            pltpu.VMEM((w.shape[1], HD), BF16),
            pltpu.VMEM((group, peers * HD), BF16),
            pltpu.VMEM((nz, 2 * HD, tok), BF16),
            pltpu.VMEM((nz, 8, tok), F32),
            pltpu.VMEM((max(nz - 1, 1), 2 * HD, tok), BF16),
            pltpu.VMEM((max(nz - 1, 1), 8, tok), F32),
            pltpu.VMEM((2, HD, tok), BF16),
            pltpu.VMEM((peers * HD, tok), BF16),
            pltpu.VMEM((6, block // 2, tok), BF16),
            pltpu.VMEM((6, block // 2, tok), BF16),
            pltpu.VMEM((block // 2, tok), F32),
            pltpu.VMEM((block // 2, tok), F32),
            pltpu.VMEM((block, tok), F32),
            pltpu.VMEM((block, tok), BF16),
            pltpu.VMEM((col, tok), BF16),
        ]
        + pair(nz - 1)
        + pair(nx - 1)
        + pair(nx - 1)
        + pair(peers - 1)
        + pair(n * (nz - 1))
        + pair(n * (nz - 1))
        + pair(n * (peers - 1))
        + pair(n * 6)
        + pair(n)
        + [dma((7,))],
        compiler_params=pltpu.CompilerParams(
            collective_id=0, has_side_effects=True, vmem_limit_bytes=56 * 1024 * 1024
        ),
        name="attend_and_project",
    )(q, k, v, dq, dk, dv, w)


def solution(mesh, dims=DIMS):
    spec = P("ctx", "fsdp")
    return jax.shard_map(
        functools.partial(call, dims),
        mesh=mesh,
        in_specs=(spec,) * 6 + (P("fsdp", None),),
        out_specs=(spec, spec),
        check_vma=False,
    )
```

```python
import functools

import jax
import jax.numpy as jnp
from jax import lax
from jax.experimental import pallas as pl
from jax.experimental.pallas import tpu as pltpu
from jax.sharding import PartitionSpec as P

MESH = pl.DeviceIdType.MESH
HD = 128
F32 = jnp.float32
BF16 = jnp.bfloat16
DIMS = (4, 4, 4, 4, 2)


def nt_dot(a, b):
    return lax.dot_general(a, b, (((1,), (1,)), ((), ())), preferred_element_type=F32)


def kernel(
    dims, chunks,
    q_ref, k_ref, v_ref, dq_ref, dk_ref, dv_ref, w_ref,
    out_ref, dout_ref,
    qd_all, kd_all, v_in, vt_own, vt_all, w_in, wt_own, wt_all,
    part, stats, part_in, stats_in, mix, x_all, send_z, recv_z, hold_a, hold_b, own, swap_out, swap_in,
    q_s, q_r, k_s, k_r, v_s, v_r, w_s, w_r, p_s, p_r, t_s, t_r, x_s, x_r, z_s, z_r, c_s, c_r, l_s,
):
    nx, nz, ny, nh, nc = dims
    tok = q_ref.shape[0]
    col = out_ref.shape[0]
    scale = 1.0 / HD**0.5
    rate = scale * 1.4426950408889634

    ctx = lax.axis_index("ctx")
    fsdp = lax.axis_index("fsdp")
    zl, x = ctx // nx, lax.rem(ctx, nx)
    core = lax.rem(fsdp, nc)
    zh = lax.rem(fsdp // nc, nh)
    y = fsdp // (nc * nh)

    def at_x(d):
        return (zl * nx + lax.rem(x + d, nx), fsdp)

    def at_zl(d):
        return (lax.rem(zl + d, nz) * nx + x, fsdp)

    def at_zh(d):
        return (ctx, (y * nh + lax.rem(zh + d, nh)) * nc + core)

    def at_yc(e):
        return (ctx, (lax.rem(y + e // nc, ny) * nh + zh) * nc + lax.rem(core + e % nc, nc))

    partners = (
        ([at_x(1), at_x(nx - 1)] if nx > 1 else [])
        + [at_zl(d) for d in range(1, nz)]
        + ([at_zh(1), at_zh(nh - 1)] if nh > 1 else [])
        + [at_yc(e) for e in range(1, ny * nc)]
    )
    barrier = pltpu.get_barrier_semaphore()
    for device in partners:
        pl.semaphore_signal(barrier, inc=1, device_id=device, device_id_type=MESH)

    def remote(src, dst, s, r, device):
        return pltpu.make_async_remote_copy(
            src_ref=src, dst_ref=dst, send_sem=s, recv_sem=r, device_id=device, device_id_type=MESH
        )

    key_rows = pl.ds(pl.multiple_of(x * tok, tok), tok)
    first, second = slice(0, HD), slice(HD, 2 * HD)
    local = [
        pltpu.make_async_copy(src, dst, l_s.at[i])
        for i, (src, dst) in enumerate(
            [
                (v_ref, v_in.at[0]),
                (dv_ref, v_in.at[1]),
                (dq_ref, qd_all.at[zl, :, first]),
                (q_ref, qd_all.at[zl, :, second]),
                (k_ref, kd_all.at[key_rows, first]),
                (dk_ref, kd_all.at[key_rows, second]),
                (w_ref, w_in),
            ]
        )
    ]
    for copy in local:
        copy.start()
    for copy in local[:2]:
        copy.wait()
    vt_own[first, :] = v_in[0].T
    vt_own[second, :] = v_in[1].T
    for copy in local[2:6]:
        copy.wait()

    pl.semaphore_wait(barrier, len(partners))

    def q_copy(d, i):
        return remote(qd_all.at[zl], qd_all.at[zl], q_s.at[i], q_r.at[i], at_zl(d))

    def q_relay(d, i):
        there = lax.rem(zl + 2, nz)
        return remote(qd_all.at[there], qd_all.at[there], q_s.at[3], q_r.at[i], at_zl(d))

    def rows_of(d):
        return pl.ds(pl.multiple_of(lax.rem(x + d, nx) * tok, tok), tok)

    def k_copy(i, d, rows):
        return remote(kd_all.at[rows], kd_all.at[rows], k_s.at[i], k_r.at[i], at_x(d))

    def v_copy(i, d):
        return remote(vt_own, vt_all.at[:, key_rows], v_s.at[i], v_r.at[i], at_x(d))

    def v_relay(i, d, rows):
        return remote(vt_all.at[:, rows], vt_all.at[:, rows], v_s.at[i], v_r.at[i], at_x(d))

    x_way = []
    if nx > 1:
        x_way = [
            k_copy(0, 1, key_rows),
            v_copy(1, nx - 1),
            v_copy(0, 1),
            k_copy(1, nx - 1, key_rows),
        ]
        for copy in x_way[:2]:
            copy.start()
    if nz > 1:
        q_copy(2, 1).start()

        @pl.when(zl != nz - 1)
        def _():
            q_copy(1, 0).start()

        @pl.when(zl != 0)
        def _():
            q_copy(3, 2).start()

    for copy in x_way[2:]:
        copy.start()
    v_local = pltpu.make_async_copy(vt_own, vt_all.at[:, key_rows], l_s.at[0])
    v_local.start()

    group = nh * nc * col
    local[6].wait()
    for i in range(ny):
        wt_own[i * group : (i + 1) * group, :] = w_in[:, i * group : (i + 1) * group].T
    slot = y * nc + core
    slot_cols = pl.ds(pl.multiple_of(slot * HD, HD), HD)

    def weight_rows(row):
        return pl.ds(pl.multiple_of(row * group, group), group)

    def w_copy(d):
        return remote(
            wt_own.at[weight_rows(lax.rem(y + d, ny))],
            wt_all.at[:, slot_cols],
            w_s.at[d],
            w_r.at[d],
            at_yc(d * nc) if d else at_yc(1),
        )

    def w_relay(d):
        there = pl.ds(pl.multiple_of((lax.rem(y + ny - d, ny) * nc + core) * HD, HD), HD)
        i = ny + d - 1
        return remote(wt_all.at[:, there], wt_all.at[:, there], w_s.at[i], w_r.at[i], at_yc(1))

    w_copies = [w_copy(d) for d in list(range(1, ny)) + [0]]
    for copy in w_copies:
        copy.start()
    w_local = pltpu.make_async_copy(wt_own.at[weight_rows(y)], wt_all.at[:, slot_cols], l_s.at[1])
    w_local.start()

    if nx > 1:
        x_way[0].wait_recv()
        x_way.append(k_copy(2, 1, rows_of(nx - 1)))
        x_way[4].start()
        x_way[1].wait_recv()
        x_way.append(v_relay(2, nx - 1, rows_of(1)))
        x_way[5].start()
    if nz > 1:
        q_copy(2, 1).wait()

        @pl.when(zl == 2)
        def _():
            q_relay(1, 2).start()

        @pl.when(zl == 1)
        def _():
            q_relay(3, 0).start()

    for copy in x_way[:2]:
        copy.wait_send()
    for copy in x_way[2:]:
        copy.wait()
    v_local.wait()
    if nz > 1:
        for d in (1, 3):
            q_copy(d, d - 1).wait_recv()

        @pl.when(zl != nz - 1)
        def _():
            q_copy(1, 0).wait_send()

        @pl.when(zl != 0)
        def _():
            q_copy(3, 2).wait_send()

        @pl.when(lax.rem(zl, nz - 1) != 0)
        def _():
            q_relay(1, 2).wait_send()

    def part_copies(c, lanes, j, device):
        i = c * (nz - 1) + j
        return (
            remote(part.at[j, :, lanes], part_in.at[j, :, lanes], p_s.at[i], p_r.at[i], device),
            remote(stats.at[j, :, lanes], stats_in.at[j, :, lanes], t_s.at[i], t_r.at[i], device),
        )

    for c, (at, size) in enumerate(chunks):
        lanes = slice(at, at + size)

        def attend(j, carry):
            owner = lax.rem(zl + j + 1, nz)
            qd = qd_all[owner, lanes, :]
            scores = nt_dot(kd_all[:, first], qd[:, second])
            steps = nt_dot(kd_all[...], qd)
            top = jnp.max(scores, axis=0, keepdims=True)
            weights = jnp.exp2((scores - top) * rate)
            spread = weights * steps
            total = jnp.sum(weights, axis=0, keepdims=True)
            mean = jnp.sum(spread, axis=0, keepdims=True) * scale / total
            low = weights.astype(BF16)
            one = jnp.dot(vt_all[...], low, preferred_element_type=F32)
            two = jnp.dot(vt_all[first, :], spread.astype(BF16), preferred_element_type=F32)
            mixed = one[first] / total
            part[j, first, lanes] = mixed.astype(BF16)
            part[j, second, lanes] = ((one[second] + two * scale) / total - mean * mixed).astype(
                BF16
            )
            stats[j, 0:1, lanes] = top * rate
            stats[j, 1:2, lanes] = total
            stats[j, 2:3, lanes] = mean
            stats[j, 3:8, lanes] = jnp.zeros((5, size), F32)

            @pl.when(j < nz - 1)
            def _():
                for copy in part_copies(c, lanes, j, (owner * nx + x, fsdp)):
                    copy.start()

            return carry

        lax.fori_loop(0, nz, attend, 0)
        if c == 0:
            for copy in w_copies:
                copy.wait()
            relays = [w_relay(d) for d in range(1, ny)]
            for copy in relays:
                copy.start()
            w_copies = relays

    block = nc * col
    slot_rows = pl.ds(pl.multiple_of(slot * HD, HD), HD)
    top_half, low_half = slice(0, block // 2), slice(block // 2, block)
    other = lax.rem(core + 1, nc)

    def merge(c):
        at, size = chunks[c]
        lanes = slice(at, at + size)
        for j in range(nz - 1):
            for copy in part_copies(c, lanes, j, at_zl(j + 1)):
                copy.wait()
        parts = [(part_in.at[j], stats_in.at[j]) for j in range(nz - 1)]
        parts.append((part.at[nz - 1], stats.at[nz - 1]))
        tops = [s[0:1, lanes] for _, s in parts]
        top = functools.reduce(jnp.maximum, tops)
        shares = [jnp.exp2(t - top) * s[1:2, lanes] for t, (_, s) in zip(tops, parts)]
        total = sum(shares)
        shares = [s / total for s in shares]
        means = [s[2:3, lanes] for _, s in parts]
        mean = sum(a * b for a, b in zip(shares, means))
        mixed = jnp.zeros((HD, size), F32)
        tangent = jnp.zeros((HD, size), F32)
        for share, here, (p, _) in zip(shares, means, parts):
            one = p[first, lanes].astype(F32)
            mixed += share * one
            tangent += share * (p[second, lanes].astype(F32) + (here - mean) * one)
        mix[0, :, lanes] = mixed.astype(BF16)
        mix[1, :, lanes] = tangent.astype(BF16)
        n = ny * nc - 1
        copies = [
            remote(
                mix.at[lax.rem(core + e % nc, nc), :, lanes],
                x_all.at[slot_rows, lanes],
                x_s.at[c * n + e - 1],
                x_r.at[c * n + e - 1],
                at_yc(e),
            )
            for e in range(1, ny * nc)
        ]
        for copy in copies:
            copy.start()
        x_all[slot_rows, lanes] = mix[core, :, lanes]
        return copies

    def z_copy(c, i, d):
        at, size = chunks[c]
        lanes = slice(at, at + size)
        k = 6 * c + i
        return remote(
            send_z.at[i, :, lanes], recv_z.at[i, :, lanes], z_s.at[k], z_r.at[k], at_zh(d)
        )

    def project(c):
        at, size = chunks[c]
        lanes = slice(at, at + size)

        def dot(d):
            rows = pl.ds(pl.multiple_of(lax.rem(zh + d, nh) * block, block), block)
            return jnp.dot(wt_all[rows, :], x_all[:, lanes], preferred_element_type=F32)

        own[:, lanes] = dot(0)
        if nh == 1:
            return []
        far = dot(2)
        send_z[0, :, lanes] = far[top_half].astype(BF16)
        send_z[1, :, lanes] = far[low_half].astype(BF16)
        copies = [z_copy(c, 0, 1), z_copy(c, 1, 3)]
        for copy in copies:
            copy.start()
        after = dot(1)
        hold_a[:, lanes] = after[top_half]
        send_z[2, :, lanes] = after[low_half].astype(BF16)
        copies.append(z_copy(c, 2, 1))
        copies[2].start()
        before = dot(3)
        hold_b[:, lanes] = before[low_half]
        send_z[3, :, lanes] = before[top_half].astype(BF16)
        copies.append(z_copy(c, 3, 3))
        copies[3].start()
        return copies

    def forward(c, copies):
        at, size = chunks[c]
        lanes = slice(at, at + size)
        for i, hold, d in ((0, hold_a, 1), (1, hold_b, 3)) if nh > 1 else ():
            copies[i].wait()
            send_z[4 + i, :, lanes] = (hold[:, lanes] + recv_z[i, :, lanes].astype(F32)).astype(
                BF16
            )
            copies.append(z_copy(c, 4 + i, d))
            copies[4 + i].start()

    def cols(i):
        return pl.ds(pl.multiple_of(i * col, col), col)

    def finish(c, copies):
        at, size = chunks[c]
        lanes = slice(at, at + size)
        for copy in copies[2:]:
            copy.wait()
        for rows, i, j in ((top_half, 3, 4), (low_half, 2, 5)):
            total = own[rows, lanes]
            if nh > 1:
                total += recv_z[i, :, lanes].astype(F32) + recv_z[j, :, lanes].astype(F32)
            swap_out[rows, lanes] = total.astype(BF16)
        copy = remote(
            swap_out.at[cols(other), lanes], swap_in.at[:, lanes], c_s.at[c], c_r.at[c], at_yc(1)
        )
        copy.start()
        return copy

    def write(c, copy):
        at, size = chunks[c]
        lanes = slice(at, at + size)
        mine = swap_out[cols(core), lanes]
        copy.wait()
        theirs = swap_in[:, lanes]
        out_ref[:, lanes] = jnp.where(core == 0, mine, theirs)
        dout_ref[:, lanes] = jnp.where(core == 0, theirs, mine)

    last = len(chunks) - 1
    sends = {}
    for c in range(last + 1):
        x_copies = merge(c)
        if c > 0:
            forward(c - 1, sends[c - 1])
        if c == 0:
            for copy in w_copies:
                copy.wait()
            w_local.wait()
        for copy in x_copies:
            copy.wait()
        sends[c] = project(c)
    swaps = {c: finish(c, sends[c]) for c in range(last)}
    forward(last, sends[last])
    for c in range(last):
        write(c, swaps[c])
    write(last, finish(last, sends[last]))


def hand_over(a_ref, b_ref, out_ref, dout_ref):
    out_ref[...] = a_ref[...]
    dout_ref[...] = b_ref[...]


def call(dims, q, k, v, dq, dk, dv, w):
    nx, nz, ny, nh, nc = dims
    tok = q.shape[0]
    col = w.shape[1] // (ny * nh * nc)
    block = nc * col
    group = nh * block
    peers = ny * nc
    chunks = ((0, HD), (HD, tok - HD))
    n = len(chunks)
    dma = pltpu.SemaphoreType.DMA
    vmem = pl.BlockSpec(memory_space=pltpu.VMEM)

    def pair(n):
        return [dma((max(n, 1),)), dma((max(n, 1),))]

    out = jax.ShapeDtypeStruct((col, tok), BF16)
    results = pl.pallas_call(
        functools.partial(kernel, dims, chunks),
        out_shape=(out, out),
        in_specs=[pl.BlockSpec(memory_space=pl.ANY)] * 7,
        out_specs=(vmem, vmem),
        scratch_shapes=[
            pltpu.VMEM((nz, tok, 2 * HD), BF16),
            pltpu.VMEM((nx * tok, 2 * HD), BF16),
            pltpu.VMEM((2, tok, HD), BF16),
            pltpu.VMEM((2 * HD, tok), BF16),
            pltpu.VMEM((2 * HD, nx * tok), BF16),
            pltpu.VMEM(w.shape, BF16),
            pltpu.VMEM((w.shape[1], HD), BF16),
            pltpu.VMEM((group, peers * HD), BF16),
            pltpu.VMEM((nz, 2 * HD, tok), BF16),
            pltpu.VMEM((nz, 8, tok), F32),
            pltpu.VMEM((max(nz - 1, 1), 2 * HD, tok), BF16),
            pltpu.VMEM((max(nz - 1, 1), 8, tok), F32),
            pltpu.VMEM((2, HD, tok), BF16),
            pltpu.VMEM((peers * HD, tok), BF16),
            pltpu.VMEM((6, block // 2, tok), BF16),
            pltpu.VMEM((6, block // 2, tok), BF16),
            pltpu.VMEM((block // 2, tok), F32),
            pltpu.VMEM((block // 2, tok), F32),
            pltpu.VMEM((block, tok), F32),
            pltpu.VMEM((block, tok), BF16),
            pltpu.VMEM((col, tok), BF16),
        ]
        + pair(4)
        + pair(3)
        + pair(3)
        + pair(2 * ny - 1)
        + pair(n * (nz - 1))
        + pair(n * (nz - 1))
        + pair(n * (peers - 1))
        + pair(n * 6)
        + pair(n)
        + [dma((7,))],
        compiler_params=pltpu.CompilerParams(
            collective_id=0, has_side_effects=True, vmem_limit_bytes=56 * 1024 * 1024
        ),
        name="attend_and_project",
    )(q, k, v, dq, dk, dv, w)
    results = pl.pallas_call(
        hand_over,
        out_shape=(out, out),
        in_specs=[vmem, vmem],
        out_specs=(vmem, vmem),
        name="hand_over",
    )(*results)
    return tuple(r.T for r in results)


def solution(mesh, dims=DIMS):
    spec = P("ctx", "fsdp")
    return jax.shard_map(
        functools.partial(call, dims),
        mesh=mesh,
        in_specs=(spec,) * 6 + (P("fsdp", None),),
        out_specs=(spec, spec),
        check_vma=False,
    )
```

```python
import functools

import jax
import jax.numpy as jnp
from jax import lax
from jax.experimental import pallas as pl
from jax.experimental.pallas import tpu as pltpu
from jax.sharding import PartitionSpec as P

MESH = pl.DeviceIdType.MESH
HD = 128
F32 = jnp.float32
BF16 = jnp.bfloat16
DIMS = (4, 4, 4, 4, 2)


def nt_dot(a, b):
    return lax.dot_general(a, b, (((1,), (1,)), ((), ())), preferred_element_type=F32)


def kernel(
    dims, chunks,
    q_ref, k_ref, v_ref, dq_ref, dk_ref, dv_ref, w_ref,
    out_ref, dout_ref,
    qd_all, kd_all, v_in, vt_own, vt_all, w_in, wt_own, wt_all,
    part, stats, part_in, stats_in, via_in, via_stats, mix, x_all, send_z, recv_z, hold_a, hold_b, own, swap_out, swap_in,
    q_s, q_r, k_s, k_r, v_s, v_r, w_s, w_r, p_s, p_r, t_s, t_r, u_r, x_s, x_r, z_s, z_r, c_s, c_r, l_s,
):
    nx, nz, ny, nh, nc = dims
    tok = q_ref.shape[0]
    col = out_ref.shape[0]
    scale = 1.0 / HD**0.5
    rate = scale * 1.4426950408889634

    ctx = lax.axis_index("ctx")
    fsdp = lax.axis_index("fsdp")
    zl, x = ctx // nx, lax.rem(ctx, nx)
    core = lax.rem(fsdp, nc)
    zh = lax.rem(fsdp // nc, nh)
    y = fsdp // (nc * nh)

    def at_x(d):
        return (zl * nx + lax.rem(x + d, nx), fsdp)

    def at_zl(d):
        return (lax.rem(zl + d, nz) * nx + x, fsdp)

    def at_zh(d):
        return (ctx, (y * nh + lax.rem(zh + d, nh)) * nc + core)

    def at_yc(e):
        return (ctx, (lax.rem(y + e // nc, ny) * nh + zh) * nc + lax.rem(core + e % nc, nc))

    partners = (
        ([at_x(1), at_x(nx - 1)] if nx > 1 else [])
        + [at_zl(d) for d in range(1, nz)]
        + ([at_zh(1), at_zh(nh - 1)] if nh > 1 else [])
        + [at_yc(e) for e in range(1, ny * nc)]
    )
    barrier = pltpu.get_barrier_semaphore()
    for device in partners:
        pl.semaphore_signal(barrier, inc=1, device_id=device, device_id_type=MESH)

    def remote(src, dst, s, r, device):
        return pltpu.make_async_remote_copy(
            src_ref=src, dst_ref=dst, send_sem=s, recv_sem=r, device_id=device, device_id_type=MESH
        )

    key_rows = pl.ds(pl.multiple_of(x * tok, tok), tok)
    first, second = slice(0, HD), slice(HD, 2 * HD)
    local = [
        pltpu.make_async_copy(src, dst, l_s.at[i])
        for i, (src, dst) in enumerate(
            [
                (v_ref, v_in.at[0]),
                (dv_ref, v_in.at[1]),
                (dq_ref, qd_all.at[zl, :, first]),
                (q_ref, qd_all.at[zl, :, second]),
                (k_ref, kd_all.at[key_rows, first]),
                (dk_ref, kd_all.at[key_rows, second]),
                (w_ref, w_in),
            ]
        )
    ]
    for copy in local:
        copy.start()
    for copy in local[:2]:
        copy.wait()
    vt_own[first, :] = v_in[0].T
    vt_own[second, :] = v_in[1].T
    for copy in local[2:6]:
        copy.wait()

    pl.semaphore_wait(barrier, len(partners))

    def q_copy(d, i):
        return remote(qd_all.at[zl], qd_all.at[zl], q_s.at[i], q_r.at[i], at_zl(d))

    def q_relay(d, i):
        there = lax.rem(zl + 2, nz)
        return remote(qd_all.at[there], qd_all.at[there], q_s.at[3], q_r.at[i], at_zl(d))

    def rows_of(d):
        return pl.ds(pl.multiple_of(lax.rem(x + d, nx) * tok, tok), tok)

    def k_copy(i, d, rows):
        return remote(kd_all.at[rows], kd_all.at[rows], k_s.at[i], k_r.at[i], at_x(d))

    def v_copy(i, d):
        return remote(vt_own, vt_all.at[:, key_rows], v_s.at[i], v_r.at[i], at_x(d))

    def v_relay(i, d, rows):
        return remote(vt_all.at[:, rows], vt_all.at[:, rows], v_s.at[i], v_r.at[i], at_x(d))

    x_way = []
    if nx > 1:
        x_way = [
            k_copy(0, 1, key_rows),
            v_copy(1, nx - 1),
            v_copy(0, 1),
            k_copy(1, nx - 1, key_rows),
        ]
        for copy in x_way[:2]:
            copy.start()
    if nz > 1:
        q_copy(2, 1).start()

        @pl.when(zl != nz - 1)
        def _():
            q_copy(1, 0).start()

        @pl.when(zl != 0)
        def _():
            q_copy(3, 2).start()

    for copy in x_way[2:]:
        copy.start()
    v_local = pltpu.make_async_copy(vt_own, vt_all.at[:, key_rows], l_s.at[0])
    v_local.start()

    group = nh * nc * col
    local[6].wait()
    for i in range(ny):
        wt_own[i * group : (i + 1) * group, :] = w_in[:, i * group : (i + 1) * group].T
    slot = y * nc + core
    slot_cols = pl.ds(pl.multiple_of(slot * HD, HD), HD)

    def weight_rows(row):
        return pl.ds(pl.multiple_of(row * group, group), group)

    def w_copy(d):
        return remote(
            wt_own.at[weight_rows(lax.rem(y + d, ny))],
            wt_all.at[:, slot_cols],
            w_s.at[d],
            w_r.at[d],
            at_yc(d * nc) if d else at_yc(1),
        )

    def w_relay(d):
        there = pl.ds(pl.multiple_of((lax.rem(y + ny - d, ny) * nc + core) * HD, HD), HD)
        i = ny + d - 1
        return remote(wt_all.at[:, there], wt_all.at[:, there], w_s.at[i], w_r.at[i], at_yc(1))

    w_copies = [w_copy(d) for d in list(range(1, ny)) + [0]]
    for copy in w_copies:
        copy.start()
    w_local = pltpu.make_async_copy(wt_own.at[weight_rows(y)], wt_all.at[:, slot_cols], l_s.at[1])
    w_local.start()

    if nx > 1:
        x_way[0].wait_recv()
        x_way.append(k_copy(2, 1, rows_of(nx - 1)))
        x_way[4].start()
        x_way[1].wait_recv()
        x_way.append(v_relay(2, nx - 1, rows_of(1)))
        x_way[5].start()
    if nz > 1:
        q_copy(2, 1).wait()

        @pl.when(zl == 2)
        def _():
            q_relay(1, 2).start()

        @pl.when(zl == 1)
        def _():
            q_relay(3, 0).start()

    for copy in x_way[:2]:
        copy.wait_send()
    for copy in x_way[2:]:
        copy.wait()
    v_local.wait()
    if nz > 1:
        for d in (1, 3):
            q_copy(d, d - 1).wait_recv()

        @pl.when(zl != nz - 1)
        def _():
            q_copy(1, 0).wait_send()

        @pl.when(zl != 0)
        def _():
            q_copy(3, 2).wait_send()

        @pl.when(lax.rem(zl, nz - 1) != 0)
        def _():
            q_relay(1, 2).wait_send()

    def part_copies(c, owner, device):
        i, k = c * nz + owner, c * nz + zl
        return (
            remote(part[c].at[owner], part_in[c].at[zl], p_s.at[i], p_r.at[k], device),
            remote(stats[c].at[owner], stats_in[c].at[zl], t_s.at[i], t_r.at[k], device),
        )

    def via_copies(c, owner, device):
        i = c * nz + owner
        return (
            remote(part[c].at[owner], via_in[c], p_s.at[i], u_r.at[c], device),
            remote(stats[c].at[owner], via_stats[c], t_s.at[i], u_r.at[len(chunks) + c], device),
        )

    def combine(parts):
        tops = [s[0:1, :] for _, s in parts]
        top = functools.reduce(jnp.maximum, tops)
        shares = [jnp.exp2(t - top) * s[1:2, :] for t, (_, s) in zip(tops, parts)]
        total = sum(shares)
        shares = [s / total for s in shares]
        means = [s[2:3, :] for _, s in parts]
        mean = sum(a * b for a, b in zip(shares, means))
        mixed = tangent = None
        for share, here, (p, _) in zip(shares, means, parts):
            one = p[first, :].astype(F32)
            two = p[second, :].astype(F32) + (here - mean) * one
            mixed = share * one if mixed is None else mixed + share * one
            tangent = share * two if tangent is None else tangent + share * two
        return mixed, tangent, top, total, mean

    at_end = lax.rem(zl, nz - 1) == 0 if nz > 1 else True
    if nz > 1:

        @pl.when(at_end)
        def _():
            for c in range(len(chunks)):
                part_in[c][nz - 1 - zl] = jnp.zeros_like(part_in[c][0])
                stats_in[c][nz - 1 - zl] = jnp.zeros_like(stats_in[c][0])
                stats_in[c][nz - 1 - zl, 0:1, :] = jnp.full_like(stats_in[c][0, 0:1, :], -1e30)

    order = (27 + 87 * ((zl + 1) // 2) + 27 * (zl // 2)) if nz > 1 else 0

    owners = [lax.rem(order // 4**j, 4) for j in range(nz)]

    def attend(c, begin, end):
        at, size = chunks[c]
        mine = owners[begin:end]
        qd = jnp.concatenate([qd_all[owner, at : at + size, :] for owner in mine], axis=0)
        scores = nt_dot(kd_all[:, first], qd[:, second])
        steps = nt_dot(kd_all[...], qd)
        top = jnp.max(scores, axis=0, keepdims=True)
        weights = jnp.exp2((scores - top) * rate)
        spread = weights * steps
        total = jnp.sum(weights, axis=0, keepdims=True)
        mean = jnp.sum(spread, axis=0, keepdims=True) * scale / total
        low = weights.astype(BF16)
        one = jnp.dot(vt_all[...], low, preferred_element_type=F32)
        two = jnp.dot(vt_all[first, :], spread.astype(BF16), preferred_element_type=F32)
        mixed = one[first] / total
        tangent = (one[second] + two * scale) / total - mean * mixed
        for i, owner in enumerate(mine):
            lanes = slice(i * size, (i + 1) * size)
            part[c][owner, first, :] = mixed[:, lanes].astype(BF16)
            part[c][owner, second, :] = tangent[:, lanes].astype(BF16)
            stats[c][owner, 0:1, :] = top[:, lanes] * rate
            stats[c][owner, 1:2, :] = total[:, lanes]
            stats[c][owner, 2:3, :] = mean[:, lanes]
            stats[c][owner, 3:8, :] = jnp.zeros((5, size), F32)
        for j in range(begin, min(end, nz - 1)):
            owner = owners[j]

            @pl.when(at_end if j == 2 else jnp.logical_not(at_end) if j == 0 else j == 1)
            def _():
                for copy in part_copies(c, owner, (owner * nx + x, fsdp)):
                    copy.start()

            if j == 0:

                @pl.when(at_end)
                def _():
                    for copy in via_copies(c, owner, ((1 + zl // 3) * nx + x, fsdp)):
                        copy.start()

    def merge_on_way(c):
        if nz == 1:
            return

        @pl.when(jnp.logical_not(at_end))
        def _():
            far = owners[2]
            for copy in via_copies(c, far, (far * nx + x, fsdp)):
                copy.wait_recv()
            mixed, tangent, top, total, mean = combine(
                [(part[c].at[far], stats[c].at[far]), (via_in[c], via_stats[c])]
            )
            part[c][far, first, :] = mixed.astype(BF16)
            part[c][far, second, :] = tangent.astype(BF16)
            stats[c][far, 0:1, :] = top
            stats[c][far, 1:2, :] = total
            stats[c][far, 2:3, :] = mean
            for copy in part_copies(c, far, (far * nx + x, fsdp)):
                copy.start()

    block = nc * col
    slot_rows = pl.ds(pl.multiple_of(slot * HD, HD), HD)
    top_half, low_half = slice(0, block // 2), slice(block // 2, block)
    other = lax.rem(core + 1, nc)

    def merge(c):
        at, size = chunks[c]
        lanes = slice(at, at + size)
        for d in range(1, nz):
            there = lax.rem(zl + d, nz)
            i = c * nz + there
            device = at_zl(d)
            copies = (
                remote(part[c].at[there], part_in[c].at[there], p_s.at[i], p_r.at[i], device),
                remote(stats[c].at[there], stats_in[c].at[there], t_s.at[i], t_r.at[i], device),
            )
            for copy in copies:
                copy.wait_send()

            @pl.when(jnp.logical_not(at_end) | (there != nz - 1 - zl))
            def _():
                for copy in copies:
                    copy.wait_recv()

        others = [lax.rem(zl + d, nz) for d in range(1, nz)]
        parts = [(part_in[c].at[i], stats_in[c].at[i]) for i in others]
        mixed, tangent, _, _, _ = combine(parts + [(part[c].at[zl], stats[c].at[zl])])
        mix[c][0] = mixed.astype(BF16)
        mix[c][1] = tangent.astype(BF16)
        n = ny * nc - 1
        copies = [
            remote(
                mix[c].at[lax.rem(core + e % nc, nc)],
                x_all[c].at[slot_rows],
                x_s.at[c * n + e - 1],
                x_r.at[c * n + e - 1],
                at_yc(e),
            )
            for e in range(1, ny * nc)
        ]
        for copy in copies:
            copy.start()
        x_all[c][slot_rows, :] = mix[c][core]
        return copies

    def z_copy(c, i, d):
        k = 6 * c + i
        return remote(send_z[c].at[i], recv_z[c].at[i], z_s.at[k], z_r.at[k], at_zh(d))

    def project(c):
        def dot(d):
            rows = pl.ds(pl.multiple_of(lax.rem(zh + d, nh) * block, block), block)
            return jnp.dot(wt_all[rows, :], x_all[c][...], preferred_element_type=F32)

        if nh == 1:
            own[c][...] = dot(0)
            return []
        copies = [z_copy(c, i, d) for i, d in enumerate((1, 3, 1, 3))]
        far = dot(2)
        send_z[c][0] = far[top_half].astype(BF16)
        send_z[c][1] = far[low_half].astype(BF16)
        after = dot(1)
        hold_a[c][...] = after[top_half]
        send_z[c][2] = after[low_half].astype(BF16)
        before = dot(3)
        hold_b[c][...] = before[low_half]
        send_z[c][3] = before[top_half].astype(BF16)
        own[c][...] = dot(0)
        return copies

    def send(copies):
        for copy in copies[:2]:
            copy.start()

    def forward(c, copies):
        at, size = chunks[c]
        lanes = slice(at, at + size)
        for copy in copies[:2]:
            copy.wait_send()
        for copy in copies[2:]:
            copy.start()
        for i, hold, d in ((0, hold_a, 1), (1, hold_b, 3)) if nh > 1 else ():
            copies[i].wait_recv()
            send_z[c][4 + i] = (hold[c][...] + recv_z[c][i].astype(F32)).astype(
                BF16
            )
            copies.append(z_copy(c, 4 + i, d))
            copies[4 + i].start()

    def cols(i):
        return pl.ds(pl.multiple_of(i * col, col), col)

    def finish(c, copies):
        at, size = chunks[c]
        lanes = slice(at, at + size)
        for copy in copies[2:]:
            copy.wait()
        for rows, i, j in ((top_half, 3, 4), (low_half, 2, 5)):
            total = own[c][rows, :]
            if nh > 1:
                total += recv_z[c][i].astype(F32) + recv_z[c][j].astype(F32)
            swap_out[c][rows, :] = total.astype(BF16)
        copy = remote(
            swap_out[c].at[cols(other)], swap_in[c], c_s.at[c], c_r.at[c], at_yc(1)
        )
        copy.start()
        return copy

    def write(c, copy):
        at, size = chunks[c]
        lanes = slice(at, at + size)
        mine = swap_out[c][cols(core), :]
        copy.wait()
        theirs = swap_in[c][...]
        out_ref[:, lanes] = jnp.where(core == 0, mine, theirs)
        dout_ref[:, lanes] = jnp.where(core == 0, theirs, mine)

    attend(0, 0, min(1, nz - 1))
    attend(0, min(1, nz - 1), min(2, nz - 1))
    attend(0, min(2, nz - 1), min(3, nz - 1))
    merge_on_way(0)
    attend(0, min(3, nz - 1), nz)
    for copy in w_copies:
        copy.wait()
    w_copies = [w_relay(d) for d in range(1, ny)]
    for copy in w_copies:
        copy.start()
    attend(1, 0, min(1, nz - 1))
    attend(1, min(1, nz - 1), min(2, nz - 1))
    attend(1, min(2, nz - 1), min(3, nz - 1))
    x_copies_0 = merge(0)
    attend(1, min(3, nz - 1), nz)
    merge_on_way(1)
    for copy in w_copies:
        copy.wait()
    w_local.wait()
    for copy in x_copies_0:
        copy.wait()
    sends_0 = project(0)
    x_copies_1 = merge(1)
    send(sends_0)
    forward(0, sends_0)
    for copy in x_copies_1:
        copy.wait()
    sends_1 = project(1)
    send(sends_1)
    swap_0 = finish(0, sends_0)
    forward(1, sends_1)
    write(0, swap_0)
    swap_1 = finish(1, sends_1)
    write(1, swap_1)


def hand_over(a_ref, b_ref, out_ref, dout_ref):
    out_ref[...] = a_ref[...]
    dout_ref[...] = b_ref[...]


def call(dims, q, k, v, dq, dk, dv, w):
    nx, nz, ny, nh, nc = dims
    tok = q.shape[0]
    col = w.shape[1] // (ny * nh * nc)
    block = nc * col
    group = nh * block
    peers = ny * nc
    chunks = ((0, HD), (HD, tok - HD))
    n = len(chunks)
    dma = pltpu.SemaphoreType.DMA
    vmem = pl.BlockSpec(memory_space=pltpu.VMEM)

    def pair(n):
        return [dma((max(n, 1),)), dma((max(n, 1),))]

    def per_chunk(shape, kind):
        return [pltpu.VMEM(shape + (size,), kind) for _, size in chunks]

    out = jax.ShapeDtypeStruct((col, tok), BF16)
    results = pl.pallas_call(
        functools.partial(kernel, dims, chunks),
        out_shape=(out, out),
        in_specs=[pl.BlockSpec(memory_space=pl.ANY)] * 7,
        out_specs=(vmem, vmem),
        scratch_shapes=[
            pltpu.VMEM((nz, tok, 2 * HD), BF16),
            pltpu.VMEM((nx * tok, 2 * HD), BF16),
            pltpu.VMEM((2, tok, HD), BF16),
            pltpu.VMEM((2 * HD, tok), BF16),
            pltpu.VMEM((2 * HD, nx * tok), BF16),
            pltpu.VMEM(w.shape, BF16),
            pltpu.VMEM((w.shape[1], HD), BF16),
            pltpu.VMEM((group, peers * HD), BF16),
            per_chunk((nz, 2 * HD), BF16),
            per_chunk((nz, 8), F32),
            per_chunk((nz, 2 * HD), BF16),
            per_chunk((nz, 8), F32),
            per_chunk((2 * HD,), BF16),
            per_chunk((8,), F32),
            per_chunk((2, HD), BF16),
            per_chunk((peers * HD,), BF16),
            per_chunk((6, block // 2), BF16),
            per_chunk((6, block // 2), BF16),
            per_chunk((block // 2,), F32),
            per_chunk((block // 2,), F32),
            per_chunk((block,), F32),
            per_chunk((block,), BF16),
            per_chunk((col,), BF16),
        ]
        + pair(4)
        + pair(3)
        + pair(3)
        + pair(2 * ny - 1)
        + pair(n * nz)
        + pair(n * nz)
        + [dma((2 * n,))]
        + pair(n * (peers - 1))
        + pair(n * 6)
        + pair(n)
        + [dma((7,))],
        compiler_params=pltpu.CompilerParams(
            collective_id=0, has_side_effects=True, vmem_limit_bytes=56 * 1024 * 1024
        ),
        name="attend_and_project",
    )(q, k, v, dq, dk, dv, w)
    results = pl.pallas_call(
        hand_over,
        out_shape=(out, out),
        in_specs=[vmem, vmem],
        out_specs=(vmem, vmem),
        name="hand_over",
    )(*results)
    return tuple(r.T for r in results)


def solution(mesh, dims=DIMS):
    spec = P("ctx", "fsdp")
    return jax.shard_map(
        functools.partial(call, dims),
        mesh=mesh,
        in_specs=(spec,) * 6 + (P("fsdp", None),),
        out_specs=(spec, spec),
        check_vma=False,
    )
```

```python
import functools

import jax
import jax.numpy as jnp
from jax import lax
from jax.experimental import pallas as pl
from jax.experimental.pallas import tpu as pltpu
from jax.sharding import PartitionSpec as P

MESH = pl.DeviceIdType.MESH
HD = 128
F32 = jnp.float32
BF16 = jnp.bfloat16
DIMS = (4, 4, 4, 4, 2)


def nt_dot(a, b):
    return lax.dot_general(a, b, (((1,), (1,)), ((), ())), preferred_element_type=F32)


def kernel(
    dims, chunks,
    q_ref, k_ref, v_ref, dq_ref, dk_ref, dv_ref, w_ref,
    out_ref, dout_ref,
    qd_all, kd_all, v_in, vt_own, vt_all, w_in, wt_own, wt_all,
    part, stats, part_in, stats_in, via_in, via_stats, mix, x_all, send_z, recv_z, hold_a, hold_b, own, swap_out, swap_in,
    q_s, q_r, k_s, k_r, v_s, v_r, w_s, w_r, p_s, p_r, t_s, t_r, u_r, x_s, x_r, z_s, z_r, c_s, c_r, l_s,
):
    nx, nz, ny, nh, nc = dims
    tok = q_ref.shape[0]
    col = out_ref.shape[0]
    scale = 1.0 / HD**0.5
    rate = scale * 1.4426950408889634

    ctx = lax.axis_index("ctx")
    fsdp = lax.axis_index("fsdp")
    zl, x = ctx // nx, lax.rem(ctx, nx)
    core = lax.rem(fsdp, nc)
    zh = lax.rem(fsdp // nc, nh)
    y = fsdp // (nc * nh)

    def at_x(d):
        return (zl * nx + lax.rem(x + d, nx), fsdp)

    def at_zl(d):
        return (lax.rem(zl + d, nz) * nx + x, fsdp)

    def at_zh(d):
        return (ctx, (y * nh + lax.rem(zh + d, nh)) * nc + core)

    def at_yc(e):
        return (ctx, (lax.rem(y + e // nc, ny) * nh + zh) * nc + lax.rem(core + e % nc, nc))

    partners = (
        ([at_x(1), at_x(nx - 1)] if nx > 1 else [])
        + [at_zl(d) for d in range(1, nz)]
        + ([at_zh(1), at_zh(nh - 1)] if nh > 1 else [])
        + [at_yc(e) for e in range(1, ny * nc)]
    )
    barrier = pltpu.get_barrier_semaphore()
    for device in partners:
        pl.semaphore_signal(barrier, inc=1, device_id=device, device_id_type=MESH)

    def remote(src, dst, s, r, device):
        return pltpu.make_async_remote_copy(
            src_ref=src, dst_ref=dst, send_sem=s, recv_sem=r, device_id=device, device_id_type=MESH
        )

    key_rows = pl.ds(pl.multiple_of(x * tok, tok), tok)
    first, second = slice(0, HD), slice(HD, 2 * HD)
    local = [
        pltpu.make_async_copy(src, dst, l_s.at[i])
        for i, (src, dst) in enumerate(
            [
                (v_ref, v_in.at[0]),
                (dv_ref, v_in.at[1]),
                (dq_ref, qd_all.at[zl, :, first]),
                (q_ref, qd_all.at[zl, :, second]),
                (k_ref, kd_all.at[key_rows, first]),
                (dk_ref, kd_all.at[key_rows, second]),
                (w_ref, w_in),
            ]
        )
    ]
    for copy in local:
        copy.start()
    for copy in local[:2]:
        copy.wait()
    vt_own[first, :] = v_in[0].T
    vt_own[second, :] = v_in[1].T
    for copy in local[2:6]:
        copy.wait()

    pl.semaphore_wait(barrier, len(partners))

    def q_copy(d, i):
        return remote(qd_all.at[zl], qd_all.at[zl], q_s.at[i], q_r.at[i], at_zl(d))

    def q_relay(d, i):
        there = lax.rem(zl + 2, nz)
        return remote(qd_all.at[there], qd_all.at[there], q_s.at[3], q_r.at[i], at_zl(d))

    def rows_of(d):
        return pl.ds(pl.multiple_of(lax.rem(x + d, nx) * tok, tok), tok)

    def k_copy(i, d, rows):
        return remote(kd_all.at[rows], kd_all.at[rows], k_s.at[i], k_r.at[i], at_x(d))

    def v_copy(i, d):
        return remote(vt_own, vt_all.at[:, key_rows], v_s.at[i], v_r.at[i], at_x(d))

    def v_relay(i, d, rows):
        return remote(vt_all.at[:, rows], vt_all.at[:, rows], v_s.at[i], v_r.at[i], at_x(d))

    x_way = []
    if nx > 1:
        x_way = [
            k_copy(0, 1, key_rows),
            v_copy(1, nx - 1),
            v_copy(0, 1),
            k_copy(1, nx - 1, key_rows),
        ]
        for copy in x_way[:2]:
            copy.start()
    if nz > 1:
        q_copy(2, 1).start()

        @pl.when(zl != nz - 1)
        def _():
            q_copy(1, 0).start()

        @pl.when(zl != 0)
        def _():
            q_copy(3, 2).start()

    for copy in x_way[2:]:
        copy.start()
    v_local = pltpu.make_async_copy(vt_own, vt_all.at[:, key_rows], l_s.at[0])
    v_local.start()

    group = nh * nc * col
    local[6].wait()
    for i in range(ny):
        wt_own[i * group : (i + 1) * group, :] = w_in[:, i * group : (i + 1) * group].T
    slot = y * nc + core
    slot_cols = pl.ds(pl.multiple_of(slot * HD, HD), HD)

    def weight_rows(row):
        return pl.ds(pl.multiple_of(row * group, group), group)

    def w_copy(d):
        return remote(
            wt_own.at[weight_rows(lax.rem(y + d, ny))],
            wt_all.at[:, slot_cols],
            w_s.at[d],
            w_r.at[d],
            at_yc(d * nc) if d else at_yc(1),
        )

    def w_relay(d):
        there = pl.ds(pl.multiple_of((lax.rem(y + ny - d, ny) * nc + core) * HD, HD), HD)
        i = ny + d - 1
        return remote(wt_all.at[:, there], wt_all.at[:, there], w_s.at[i], w_r.at[i], at_yc(1))

    w_copies = [w_copy(d) for d in list(range(1, ny)) + [0]]
    for copy in w_copies:
        copy.start()
    w_local = pltpu.make_async_copy(wt_own.at[weight_rows(y)], wt_all.at[:, slot_cols], l_s.at[1])
    w_local.start()

    if nx > 1:
        x_way[0].wait_recv()
        x_way.append(k_copy(2, 1, rows_of(nx - 1)))
        x_way[4].start()
        x_way[1].wait_recv()
        x_way.append(v_relay(2, nx - 1, rows_of(1)))
        x_way[5].start()
    if nz > 1:
        q_copy(2, 1).wait()

        @pl.when(zl == 2)
        def _():
            q_relay(1, 2).start()

        @pl.when(zl == 1)
        def _():
            q_relay(3, 0).start()

    for copy in x_way[:2]:
        copy.wait_send()
    for copy in x_way[2:]:
        copy.wait()
    v_local.wait()
    if nz > 1:
        for d in (1, 3):
            q_copy(d, d - 1).wait_recv()

        @pl.when(zl != nz - 1)
        def _():
            q_copy(1, 0).wait_send()

        @pl.when(zl != 0)
        def _():
            q_copy(3, 2).wait_send()

        @pl.when(lax.rem(zl, nz - 1) != 0)
        def _():
            q_relay(1, 2).wait_send()

    def part_copies(c, owner, device):
        i, k = c * nz + owner, c * nz + zl
        return (
            remote(part[c].at[owner], part_in[c].at[zl], p_s.at[i], p_r.at[k], device),
            remote(stats[c].at[owner], stats_in[c].at[zl], t_s.at[i], t_r.at[k], device),
        )

    def via_copies(c, owner, device):
        i = c * nz + owner
        return (
            remote(part[c].at[owner], via_in[c], p_s.at[i], u_r.at[c], device),
            remote(stats[c].at[owner], via_stats[c], t_s.at[i], u_r.at[len(chunks) + c], device),
        )

    def combine(parts):
        tops = [s[0:1, :] for _, s in parts]
        top = functools.reduce(jnp.maximum, tops)
        shares = [jnp.exp2(t - top) * s[1:2, :] for t, (_, s) in zip(tops, parts)]
        total = sum(shares)
        shares = [s / total for s in shares]
        means = [s[2:3, :] for _, s in parts]
        mean = sum(a * b for a, b in zip(shares, means))
        mixed = tangent = None
        for share, here, (p, _) in zip(shares, means, parts):
            one = p[first, :].astype(F32)
            two = p[second, :].astype(F32) + (here - mean) * one
            mixed = share * one if mixed is None else mixed + share * one
            tangent = share * two if tangent is None else tangent + share * two
        return mixed, tangent, top, total, mean

    at_end = lax.rem(zl, nz - 1) == 0 if nz > 1 else True
    if nz > 1:

        @pl.when(at_end)
        def _():
            for c in range(len(chunks)):
                part_in[c][nz - 1 - zl] = jnp.zeros_like(part_in[c][0])
                stats_in[c][nz - 1 - zl] = jnp.zeros_like(stats_in[c][0])
                stats_in[c][nz - 1 - zl, 0:1, :] = jnp.full_like(stats_in[c][0, 0:1, :], -1e30)

    order = (27 + 87 * ((zl + 1) // 2) + 27 * (zl // 2)) if nz > 1 else 0

    owners = [lax.rem(order // 4**j, 4) for j in range(nz)]

    def attend(c, begin, end):
        at, size = chunks[c]
        mine = owners[begin:end]
        qd = jnp.concatenate([qd_all[owner, at : at + size, :] for owner in mine], axis=0)
        scores = nt_dot(kd_all[:, first], qd[:, second])
        steps = nt_dot(kd_all[...], qd)
        top = jnp.max(scores, axis=0, keepdims=True)
        weights = jnp.exp2((scores - top) * rate)
        spread = weights * steps
        total = jnp.sum(weights, axis=0, keepdims=True)
        mean = jnp.sum(spread, axis=0, keepdims=True) * scale / total
        low = weights.astype(BF16)
        one = jnp.dot(vt_all[...], low, preferred_element_type=F32)
        two = jnp.dot(vt_all[first, :], spread.astype(BF16), preferred_element_type=F32)
        mixed = one[first] / total
        tangent = (one[second] + two * scale) / total - mean * mixed
        for i, owner in enumerate(mine):
            lanes = slice(i * size, (i + 1) * size)
            part[c][owner, first, :] = mixed[:, lanes].astype(BF16)
            part[c][owner, second, :] = tangent[:, lanes].astype(BF16)
            stats[c][owner, 0:1, :] = top[:, lanes] * rate
            stats[c][owner, 1:2, :] = total[:, lanes]
            stats[c][owner, 2:3, :] = mean[:, lanes]
            stats[c][owner, 3:8, :] = jnp.zeros((5, size), F32)
        for j in range(begin, min(end, nz - 1)):
            owner = owners[j]

            @pl.when(at_end if j == 2 else jnp.logical_not(at_end) if j == 0 else j == 1)
            def _():
                for copy in part_copies(c, owner, (owner * nx + x, fsdp)):
                    copy.start()

            if j == 0:

                @pl.when(at_end)
                def _():
                    for copy in via_copies(c, owner, ((1 + zl // 3) * nx + x, fsdp)):
                        copy.start()

    def merge_on_way(c):
        if nz == 1:
            return

        @pl.when(jnp.logical_not(at_end))
        def _():
            far = owners[2]
            for copy in via_copies(c, far, (far * nx + x, fsdp)):
                copy.wait_recv()
            mixed, tangent, top, total, mean = combine(
                [(part[c].at[far], stats[c].at[far]), (via_in[c], via_stats[c])]
            )
            part[c][far, first, :] = mixed.astype(BF16)
            part[c][far, second, :] = tangent.astype(BF16)
            stats[c][far, 0:1, :] = top
            stats[c][far, 1:2, :] = total
            stats[c][far, 2:3, :] = mean
            for copy in part_copies(c, far, (far * nx + x, fsdp)):
                copy.start()

    block = nc * col
    slot_rows = pl.ds(pl.multiple_of(slot * HD, HD), HD)
    top_half, low_half = slice(0, block // 2), slice(block // 2, block)
    other = lax.rem(core + 1, nc)

    def merge(c):
        at, size = chunks[c]
        lanes = slice(at, at + size)
        for d in range(1, nz):
            there = lax.rem(zl + d, nz)
            i = c * nz + there
            device = at_zl(d)
            copies = (
                remote(part[c].at[there], part_in[c].at[there], p_s.at[i], p_r.at[i], device),
                remote(stats[c].at[there], stats_in[c].at[there], t_s.at[i], t_r.at[i], device),
            )
            for copy in copies:
                copy.wait_send()

            @pl.when(jnp.logical_not(at_end) | (there != nz - 1 - zl))
            def _():
                for copy in copies:
                    copy.wait_recv()

        others = [lax.rem(zl + d, nz) for d in range(1, nz)]
        parts = [(part_in[c].at[i], stats_in[c].at[i]) for i in others]
        mixed, tangent, _, _, _ = combine(parts + [(part[c].at[zl], stats[c].at[zl])])
        mix[c][0] = mixed.astype(BF16)
        mix[c][1] = tangent.astype(BF16)
        n = ny * nc - 1
        copies = [
            remote(
                mix[c].at[lax.rem(core + e % nc, nc)],
                x_all[c].at[slot_rows],
                x_s.at[c * n + e - 1],
                x_r.at[c * n + e - 1],
                at_yc(e),
            )
            for e in range(1, ny * nc)
        ]
        for copy in copies:
            copy.start()
        x_all[c][slot_rows, :] = mix[c][core]
        return copies

    def z_copy(c, i, d):
        k = 6 * c + i
        return remote(send_z[c].at[i], recv_z[c].at[i], z_s.at[k], z_r.at[k], at_zh(d))

    def project(c):
        def dot(d):
            rows = pl.ds(pl.multiple_of(lax.rem(zh + d, nh) * block, block), block)
            return jnp.dot(wt_all[rows, :], x_all[c][...], preferred_element_type=F32)

        if nh == 1:
            own[c][...] = dot(0)
            return []
        copies = [z_copy(c, i, d) for i, d in enumerate((1, 3, 1, 3))]
        far = dot(2)
        send_z[c][0] = far[top_half].astype(BF16)
        send_z[c][1] = far[low_half].astype(BF16)
        after = dot(1)
        hold_a[c][...] = after[top_half]
        send_z[c][2] = after[low_half].astype(BF16)
        before = dot(3)
        hold_b[c][...] = before[low_half]
        send_z[c][3] = before[top_half].astype(BF16)
        own[c][...] = dot(0)
        return copies

    def send(copies):
        for copy in copies[:2]:
            copy.start()

    def forward(c, copies):
        at, size = chunks[c]
        lanes = slice(at, at + size)
        for copy in copies[:2]:
            copy.wait_send()
        for copy in copies[2:]:
            copy.start()
        for i, hold, d in ((0, hold_a, 1), (1, hold_b, 3)) if nh > 1 else ():
            copies[i].wait_recv()
            send_z[c][4 + i] = (hold[c][...] + recv_z[c][i].astype(F32)).astype(
                BF16
            )
            copies.append(z_copy(c, 4 + i, d))
            copies[4 + i].start()

    def cols(i):
        return pl.ds(pl.multiple_of(i * col, col), col)

    def finish(c, copies):
        at, size = chunks[c]
        lanes = slice(at, at + size)
        for copy in copies[2:]:
            copy.wait()
        for rows, i, j in ((top_half, 3, 4), (low_half, 2, 5)):
            total = own[c][rows, :]
            if nh > 1:
                total += recv_z[c][i].astype(F32) + recv_z[c][j].astype(F32)
            swap_out[c][rows, :] = total.astype(BF16)
        copy = remote(
            swap_out[c].at[cols(other)], swap_in[c], c_s.at[c], c_r.at[c], at_yc(1)
        )
        copy.start()
        return copy

    def write(c, copy):
        at, size = chunks[c]
        lanes = slice(at, at + size)
        mine = swap_out[c][cols(core), :]
        copy.wait()
        theirs = swap_in[c][...]
        out_ref[:, lanes] = jnp.where(core == 0, mine, theirs)
        dout_ref[:, lanes] = jnp.where(core == 0, theirs, mine)

    attend(0, 0, min(1, nz - 1))
    attend(0, min(1, nz - 1), min(2, nz - 1))
    attend(0, min(2, nz - 1), min(3, nz - 1))
    attend(0, min(3, nz - 1), nz)
    merge_on_way(0)
    for copy in w_copies:
        copy.wait()
    w_copies = [w_relay(d) for d in range(1, ny)]
    for copy in w_copies:
        copy.start()
    attend(1, 0, min(1, nz - 1))
    attend(1, min(1, nz - 1), min(2, nz - 1))
    attend(1, min(2, nz - 1), min(3, nz - 1))
    x_copies_0 = merge(0)
    attend(1, min(3, nz - 1), nz)
    merge_on_way(1)
    for copy in w_copies:
        copy.wait()
    w_local.wait()
    for copy in x_copies_0:
        copy.wait()
    sends_0 = project(0)
    x_copies_1 = merge(1)
    send(sends_0)
    forward(0, sends_0)
    for copy in x_copies_1:
        copy.wait()
    sends_1 = project(1)
    send(sends_1)
    swap_0 = finish(0, sends_0)
    forward(1, sends_1)
    write(0, swap_0)
    swap_1 = finish(1, sends_1)
    write(1, swap_1)


def hand_over(a_ref, b_ref, out_ref, dout_ref):
    out_ref[...] = a_ref[...]
    dout_ref[...] = b_ref[...]


def call(dims, q, k, v, dq, dk, dv, w):
    nx, nz, ny, nh, nc = dims
    tok = q.shape[0]
    col = w.shape[1] // (ny * nh * nc)
    block = nc * col
    group = nh * block
    peers = ny * nc
    chunks = ((0, HD), (HD, tok - HD))
    n = len(chunks)
    dma = pltpu.SemaphoreType.DMA
    vmem = pl.BlockSpec(memory_space=pltpu.VMEM)

    def pair(n):
        return [dma((max(n, 1),)), dma((max(n, 1),))]

    def per_chunk(shape, kind):
        return [pltpu.VMEM(shape + (size,), kind) for _, size in chunks]

    out = jax.ShapeDtypeStruct((col, tok), BF16)
    results = pl.pallas_call(
        functools.partial(kernel, dims, chunks),
        out_shape=(out, out),
        in_specs=[pl.BlockSpec(memory_space=pl.ANY)] * 7,
        out_specs=(vmem, vmem),
        scratch_shapes=[
            pltpu.VMEM((nz, tok, 2 * HD), BF16),
            pltpu.VMEM((nx * tok, 2 * HD), BF16),
            pltpu.VMEM((2, tok, HD), BF16),
            pltpu.VMEM((2 * HD, tok), BF16),
            pltpu.VMEM((2 * HD, nx * tok), BF16),
            pltpu.VMEM(w.shape, BF16),
            pltpu.VMEM((w.shape[1], HD), BF16),
            pltpu.VMEM((group, peers * HD), BF16),
            per_chunk((nz, 2 * HD), BF16),
            per_chunk((nz, 8), F32),
            per_chunk((nz, 2 * HD), BF16),
            per_chunk((nz, 8), F32),
            per_chunk((2 * HD,), BF16),
            per_chunk((8,), F32),
            per_chunk((2, HD), BF16),
            per_chunk((peers * HD,), BF16),
            per_chunk((6, block // 2), BF16),
            per_chunk((6, block // 2), BF16),
            per_chunk((block // 2,), F32),
            per_chunk((block // 2,), F32),
            per_chunk((block,), F32),
            per_chunk((block,), BF16),
            per_chunk((col,), BF16),
        ]
        + pair(4)
        + pair(3)
        + pair(3)
        + pair(2 * ny - 1)
        + pair(n * nz)
        + pair(n * nz)
        + [dma((2 * n,))]
        + pair(n * (peers - 1))
        + pair(n * 6)
        + pair(n)
        + [dma((7,))],
        compiler_params=pltpu.CompilerParams(
            collective_id=0, has_side_effects=True, vmem_limit_bytes=56 * 1024 * 1024
        ),
        name="attend_and_project",
    )(q, k, v, dq, dk, dv, w)
    results = pl.pallas_call(
        hand_over,
        out_shape=(out, out),
        in_specs=[vmem, vmem],
        out_specs=(vmem, vmem),
        name="hand_over",
    )(*results)
    return tuple(r.T for r in results)


def solution(mesh, dims=DIMS):
    spec = P("ctx", "fsdp")
    return jax.shard_map(
        functools.partial(call, dims),
        mesh=mesh,
        in_specs=(spec,) * 6 + (P("fsdp", None),),
        out_specs=(spec, spec),
        check_vma=False,
    )
```
